32 devices in a mesh: dp: 4 (over y, core), expert: 8 (over z, x).
Axes of the slice: x: 2, y: 2, z: 4, core: 2. Of those that a mesh axis runs over, the one named last changes fastest.
Arguments:
- out_grad: bfloat16 [4096, 7168], P(('dp', 'expert')), may hold values from -6 to 6
- gate_weights: bfloat16 [4096, 8], P(('dp', 'expert')), may hold values from 0.099609375 to 1
- routes: int32 [4096, 8], P(('dp', 'expert')), may hold values from 0 to 63, all different within a row; in each aligned block of 128 rows (0 to 127, 128 to 255, ...) at most 24 rows name the same one
- seq_ids: int32 [32, 128], P(('dp', 'expert')), may hold values from 0 to 1, never falling along the last dimension, each value on 1 to 96 neighbouring positions
- hidden: bfloat16 [32, 64, 24, 2048], P('dp', 'expert'), may hold values from -6 to 6
- proj_out: bfloat16 [7168, 128], P('expert'), may hold values from -0.0625 to 0.0625
- proj_in: bfloat16 [2048, 32], P('dp'), may hold values from -0.125 to 0.125
Outputs:
- seq_grads: bfloat16 [64, 64, 4096], P('dp', 'expert')
The draws below stay inside these ranges and needn't reach their ends.
Inputs may be any that keep to these rules, and one draw needn't show every extreme that they name: `routes`: in the rows of one device (aligned blocks of 128 tokens) no expert is named by more than 24 rows, a bound that some block reaches; a token names 8 different experts. `seq_ids`: within each block never falling; every id of 0 to 1 occurs, no sequence has more than 96 tokens.
All inputs are finite; a program needn't handle non-finite values.
Results may differ from the reference program's by a relative error of at most 0.0085.
Values may be sent and summed in bfloat16 or wider, within the bound.
A program may use at most 128 MiB of HBM per device.

```python
import math
import jax
import jax.numpy as jnp
import numpy as np
from jax import lax

D = 7168
FF = 2048
TOP = 8
TOK_DEV = 128
SEQ_DEV = 2
K_OUT = 128
K_IN = 32
EXPERTS = 64
CAP = 24
BLOCKS = 32
TOKENS = 4096
SEQS = 64
SEG_MOST = 96


def shard_levels(key, dims, pieces, low, high):
    factor_of, own = 1.0, jax.random.fold_in(key, 6)
    for dim, parts in pieces:
        steps = jnp.exp(jax.random.uniform(jax.random.fold_in(own, dim), (parts,), jnp.float32, low / len(pieces), high / len(pieces)))
        factor_of = factor_of * jnp.repeat(steps, dims[dim] // parts).reshape([-1 if axis == dim else 1 for axis in range(len(dims))])
    return factor_of


def length_profile(amount, total, limit, skew):
    weights = [(1 << 20) // math.isqrt(rank ** skew) + 1 for rank in range(2, amount + 1)]
    rest, holding = total - limit - (amount - 1), [1] * (amount - 1)
    while rest > 0:
        candidates = [i for i in range(amount - 1) if holding[i] < limit]
        whole, budget = sum([weights[i] for i in candidates]), rest
        for i in candidates:
            extra = min(limit - holding[i], max(1, budget * weights[i] // whole), rest)
            holding[i] = holding[i] + extra
            rest = rest - extra
    return np.array([limit] + holding)


def uneven(key, amount, total, most, lean):
    if amount == 2:
        one = jax.random.randint(key, (), max(1, total - most), min(most, total - 1) + 1)
        return jnp.stack([one, total - one])
    sizes = jnp.asarray(length_profile(amount, total, most, lean), jnp.int32)
    couples = (amount - 1) // 2
    giver, receiver = sizes[1:1 + 2 * couples:2], sizes[2:2 + 2 * couples:2]
    slack = jnp.minimum(giver - 1, most - receiver)
    passed = jax.random.randint(jax.random.fold_in(key, 1), (couples,), 0, 1 << 20) % (slack + 1)
    sizes = sizes.at[1:1 + 2 * couples:2].set(giver - passed).at[2:2 + 2 * couples:2].set(receiver + passed)
    return sizes[jax.random.permutation(jax.random.fold_in(key, 2), amount)]


def routed_block(stream_key, own, number, rows, count, top, most, skew):
    ranking = jax.random.permutation(stream_key, count)
    packed, usual = shares(count, rows * top, most, skew, True), shares(count, rows * top, most, skew, False)
    places = jnp.arange(count)

    def named(tallies, turn):
        used = int((tallies > 0).sum())
        fixed = max(1, used // 4)
        moved = fixed + (places - fixed + turn * (used - fixed)) % max(1, count - fixed)
        return jnp.zeros((count,), jnp.int32).at[ranking[jnp.where(places < fixed, places, moved)]].set(jnp.asarray(tallies, jnp.int32))

    tallies = jnp.where(number % 4 == 0, named(packed, number // 4), named(usual, number - number // 4 - 1))
    mixed = jax.random.permutation(jax.random.fold_in(own, 3), count)
    source_of, sink = mixed[0:count // 2 * 2:2], mixed[1:count // 2 * 2:2]
    margin = jnp.minimum(tallies[source_of] - 1, most - tallies[sink]) // 2
    margin = jnp.where((source_of == ranking[0]) | (sink == ranking[0]) | (tallies[sink] == 0), 0, jnp.maximum(margin, 0))
    moved = jax.random.randint(jax.random.fold_in(own, 4), (count // 2,), 0, 1 << 20) % (margin + 1)
    tallies = tallies.at[source_of].add(-moved).at[sink].add(moved)
    items = jnp.searchsorted(jnp.cumsum(tallies), jnp.arange(rows * top), side="right").astype(jnp.int32)
    grid = items.reshape(top, rows).T
    grid = grid[jax.random.permutation(jax.random.fold_in(own, 1), rows)]
    turn = jax.random.randint(jax.random.fold_in(own, 2), (rows, 1), 0, top)
    return jnp.take_along_axis(grid, (jnp.arange(top)[None, :] + turn) % top, axis=1)


def shares(count, total, reach, slope, full):
    loads = [(1 << 20) // math.isqrt(rank ** slope) + 1 for rank in range(1, count + 1)]
    largest = reach if full else min(reach, max(-(-total // count), total * loads[0] // sum(loads)))
    least = 1 if total - largest >= count - 1 else 0
    given, rest = [largest] + [least] * (count - 1), total - largest - least * (count - 1)
    while rest > 0:
        free = [i for i in range(1, count) if given[i] < largest] or [i for i in range(1, count) if given[i] < reach]
        mass, remaining = sum([loads[i] for i in free]), rest
        for i in free:
            extra = min(reach - given[i], max(1, remaining * loads[i] // mass), rest)
            given[i] = given[i] + extra
            rest = rest - extra
    return np.array(given)


def normal_values(key, shape, deviation, limit, split=(), kind=jnp.bfloat16):
    result = deviation * jax.random.normal(key, shape, jnp.float32)
    if split:
        result = result * shard_levels(key, shape, split, -0.22, 0.18)
    return jnp.clip(result, -limit, limit).astype(kind)


def setup_inputs(seed: int = 0) -> dict:
    keys = jax.random.split(jax.random.key(seed), 8)
    out_grad = normal_values(keys[0], (TOKENS, D), 1.0, 6.0, ((0, 32),))
    gate_weights = jnp.clip(jnp.exp(math.log(1.0) - 2.306499 * jax.random.uniform(keys[1], (TOKENS, TOP), jnp.float32) ** shard_levels(keys[1], (TOKENS, TOP), ((0, 32),), -0.2, 0.2)), 0.099609375, 1.0).astype(jnp.bfloat16)
    routes_keys = jax.random.split(jax.random.fold_in(keys[2], 1), TOKENS // TOK_DEV)
    routes_turns = jax.random.permutation(jax.random.fold_in(keys[2], 3), TOKENS // TOK_DEV)
    routes = jax.vmap(lambda own, number: routed_block(jax.random.fold_in(keys[2], 2), own, number, TOK_DEV, EXPERTS, TOP, CAP, 2))(routes_keys, routes_turns).reshape((TOKENS, TOP))
    seq_ids = jax.vmap(lambda own: jnp.searchsorted(jnp.cumsum(uneven(own, SEQ_DEV, TOK_DEV, SEG_MOST, 1)), jnp.arange(TOK_DEV), side="right"))(jax.random.split(keys[3], BLOCKS)).reshape((BLOCKS, TOK_DEV)).astype(jnp.int32)
    hidden = normal_values(keys[4], (BLOCKS, EXPERTS, CAP, FF), 1.0, 6.0, ((0, 4), (1, 8)))
    proj_out = normal_values(keys[5], (D, K_OUT), D ** -0.5, 0.0625, ((0, 8),))
    proj_in = normal_values(keys[6], (FF, K_IN), FF ** -0.5, 0.125, ((0, 4),))
    return {"out_grad": out_grad, "gate_weights": gate_weights, "routes": routes, "seq_ids": seq_ids, "hidden": hidden, "proj_out": proj_out, "proj_in": proj_in}


def assign_slots(routes, experts):
    flat_routes = routes.reshape(-1)
    one_hot = (flat_routes[:, None] == jnp.arange(experts, dtype=jnp.int32)[None, :]).astype(jnp.int32)
    earlier = jnp.cumsum(one_hot, axis=0) - one_hot
    return jnp.sum(earlier * one_hot, axis=1).astype(jnp.int32)


def pair_sums(grad_rows, hidden_rows, weights, segment, count):
    outer = (weights.astype(jnp.float32)[:, None, None] * grad_rows.astype(jnp.float32)[:, :, None]) * hidden_rows.astype(jnp.float32)[:, None, :]
    return jax.ops.segment_sum(outer.reshape(outer.shape[0], -1), segment, num_segments=count)


def reference(out_grad, gate_weights, routes, seq_ids, hidden, proj_out, proj_in):
    def one_block(block_items):
        grad_block, gate_block, route_block, seq_row, stored = block_items
        grad_proj = jnp.dot(grad_block, proj_out, preferred_element_type=jnp.float32).astype(jnp.bfloat16)
        flat_routes = route_block.reshape(-1)
        positions = (flat_routes * CAP + assign_slots(route_block, EXPERTS)).astype(jnp.int32)
        stored_rows = stored.reshape(EXPERTS * CAP, FF)[positions]
        hidden_proj = jnp.dot(stored_rows, proj_in, preferred_element_type=jnp.float32).astype(jnp.bfloat16)
        owners = jnp.repeat(jnp.arange(TOK_DEV, dtype=jnp.int32), TOP)
        segment = (seq_row[owners] * EXPERTS + flat_routes).astype(jnp.int32)
        totals = pair_sums(grad_proj[owners], hidden_proj, gate_block.reshape(-1), segment, SEQ_DEV * EXPERTS)
        return totals.reshape(SEQ_DEV, EXPERTS, K_OUT * K_IN).astype(jnp.bfloat16)

    per_block = lax.map(one_block, (out_grad.reshape(BLOCKS, TOK_DEV, D), gate_weights.reshape(BLOCKS, TOK_DEV, TOP), routes.reshape(BLOCKS, TOK_DEV, TOP), seq_ids, hidden))
    return per_block.reshape(SEQS, EXPERTS, K_OUT * K_IN)
```

```python
import functools

import jax
import jax.numpy as jnp
from jax import lax
from jax.experimental import pallas as pl
from jax.experimental.pallas import tpu as pltpu
from jax.sharding import PartitionSpec as P

SEQ_DEV = 2
LANES = 128
MESH = pl.DeviceIdType.MESH
F32 = jnp.float32
BF16 = jnp.bfloat16


def iota(shape, dim):
    return lax.broadcasted_iota(jnp.int32, shape, dim)


def dot(a, b):
    return jnp.dot(a, b, preferred_element_type=F32)


def dot_nt(a, b):
    return lax.dot_general(a, b, (((1,), (1,)), ((), ())), preferred_element_type=F32)


def kernel(
    nd, ne, cap,
    og_hbm, gate_hbm, routes_hbm, seq_hbm, hid_hbm, po_hbm, pi_hbm, out_hbm,
    og, gate, routes, seq, hid, pall, pin, pin_all, pin4, tbl_mine, tbl_all, g_all,
    hp, pick, bd, stage, outv,
    og_sem, small_sem, hid_sem, po_sem, ring_send, ring_recv, sib_send, sib_recv,
    pin_send, pin_recv, tbl_send, tbl_recv, g_send, g_recv, out_sem,
):
    tokens = og.shape[0]
    shard = po_hbm.shape[0]
    k_out = po_hbm.shape[1]
    k_in = pi_hbm.shape[1]
    top = routes.shape[1]
    rows = hp.shape[1]
    local = rows // cap
    experts = ne * local
    quads = LANES // k_in
    groups = k_out // quads
    half = shard // 2
    cut = half // 32 * 16
    parts = ((0, cut), (cut, half - cut))
    far = ne // 2

    dp = lax.axis_index("dp")
    me = lax.axis_index("expert")
    core = lax.rem(dp, 2)
    sibling = dp + 1 - 2 * core
    odd = lax.rem(me, 2)
    here = (1 - odd) * (me // 2) + odd * (ne - 1 - me // 2)

    def at(place):
        place = lax.rem(place + 2 * ne, ne)
        back = place // (ne // 2)
        return (1 - back) * (2 * place) + back * (2 * (ne - 1 - place) + 1)

    small = [
        pltpu.make_async_copy(pi_hbm, pin, small_sem.at[0]),
        pltpu.make_async_copy(routes_hbm, routes, small_sem.at[1]),
        pltpu.make_async_copy(gate_hbm, gate, small_sem.at[2]),
        pltpu.make_async_copy(seq_hbm, seq, small_sem.at[3]),
    ]
    own_rows = pl.ds(pl.multiple_of(me * shard, 16), shard)
    own = pltpu.make_async_copy(po_hbm, pall.at[own_rows, :], po_sem)
    grads = pltpu.make_async_copy(og_hbm, og, og_sem)
    for copy in small:
        copy.start()
    own.start()
    grads.start()

    def hidden_copy(b):
        return pltpu.make_async_copy(
            hid_hbm.at[pl.ds(b * rows, rows), :], hid.at[b], hid_sem.at[b]
        )

    for b in range(ne):
        hidden_copy(b).start()

    barrier = pltpu.get_barrier_semaphore()
    for k in range(1, ne):
        pl.semaphore_signal(
            barrier, inc=1, device_id=(dp, lax.rem(me + k, ne)), device_id_type=MESH
        )
    for k in range(1, nd):
        pl.semaphore_signal(
            barrier, inc=1, device_id=(lax.rem(dp + k, nd), me), device_id_type=MESH
        )
    pl.semaphore_wait(barrier, ne + nd - 2)

    def step(way):
        return 1 - 2 * way

    def uses(way, d):
        return (0, 1) if d < far else (way,)

    def span(source, part, side):
        first, size = parts[part]
        return pl.ds(pl.multiple_of(source * shard + side * half + first, 16), size)

    def ring(way, d, part):
        source = at(here - step(way) * (d - 1))
        first, size = parts[part]
        if d == 1:
            src = po_hbm.at[pl.ds(pl.multiple_of(core * half + first, 16), size), :]
        else:
            src = pall.at[span(source, part, core), :]
        return pltpu.make_async_remote_copy(
            src_ref=src,
            dst_ref=pall.at[span(source, part, core), :],
            send_sem=ring_send.at[way, d - 1, part],
            recv_sem=ring_recv.at[way, d - 1, part],
            device_id=(dp, at(here + step(way))),
            device_id_type=MESH,
        )

    def ring_arrival(way, d, part):
        source = at(here - step(way) * d)
        block = pall.at[span(source, part, core), :]
        return pltpu.make_async_remote_copy(
            src_ref=block,
            dst_ref=block,
            send_sem=ring_send.at[way, d - 1, part],
            recv_sem=ring_recv.at[way, d - 1, part],
            device_id=(dp, at(here + step(way))),
            device_id_type=MESH,
        )

    def hand_over(way, d, part, side):
        source = at(here - step(way) * d)
        block = pall.at[span(source, part, side), :]
        return pltpu.make_async_remote_copy(
            src_ref=block,
            dst_ref=block,
            send_sem=sib_send.at[way, d - 1, part],
            recv_sem=sib_recv.at[way, d - 1, part],
            device_id=(sibling, me),
            device_id_type=MESH,
        )

    def relay(d):
        for part in (0, 1):
            for way in (0, 1):
                if part in uses(way, d):
                    ring_arrival(way, d, part).wait_recv()
                    if d < far and part in uses(way, d + 1):
                        ring(way, d + 1, part).start()
                    hand_over(way, d, part, core).start()

    def handed(d):
        for way in (0, 1):
            for part in uses(way, d):
                hand_over(way, d, part, 1 - core).wait_recv()

    for part in (0, 1):
        for way in (0, 1):
            ring(way, 1, part).start()

    def pin_copy(k):
        return pltpu.make_async_remote_copy(
            src_ref=pin_all.at[dp],
            dst_ref=pin_all.at[dp],
            send_sem=pin_send.at[k - 1],
            recv_sem=pin_recv.at[k - 1],
            device_id=(lax.rem(dp + k, nd), me),
            device_id_type=MESH,
        )

    def pin_arrival(k):
        block = pin_all.at[lax.rem(dp + nd - k, nd)]
        return pltpu.make_async_remote_copy(
            src_ref=block,
            dst_ref=block,
            send_sem=pin_send.at[k - 1],
            recv_sem=pin_recv.at[k - 1],
            device_id=(lax.rem(dp + k, nd), me),
            device_id_type=MESH,
        )

    small[0].wait()
    eye = (iota((k_in, k_in), 0) == iota((k_in, k_in), 1)).astype(F32).astype(BF16)
    pin_all[dp] = dot_nt(eye, pin[...]).astype(BF16)
    for k in range(1, nd):
        pin_copy(k).start()

    def exchange(buffer, sends, receives, k, mine):
        if mine:
            src, dst = buffer
        else:
            dst = buffer[1]
            src = dst
        return pltpu.make_async_remote_copy(
            src_ref=src,
            dst_ref=dst,
            send_sem=sends.at[k - 1],
            recv_sem=receives.at[k - 1],
            device_id=(dp, lax.rem(me + k, ne)),
            device_id_type=MESH,
        )

    def table_copy(k):
        return exchange(
            (tbl_mine.at[lax.rem(me + k, ne)], tbl_all.at[me]), tbl_send, tbl_recv, k, True
        )

    def table_arrival(k):
        return exchange(
            (None, tbl_all.at[lax.rem(me + ne - k, ne)]), tbl_send, tbl_recv, k, False
        )

    for copy in small[1:]:
        copy.wait()
    eye_top = (iota((top, top), 0) == iota((top, top), 1)).astype(F32).astype(BF16)
    routes_t = dot_nt(eye_top, routes[...].astype(F32).astype(BF16))
    gates_t = dot_nt(eye_top, gate[...])
    number = iota((experts, tokens), 0)
    number_f = number.astype(F32)
    named = jnp.zeros((experts, tokens), F32)
    weight = jnp.zeros((experts, tokens), F32)
    for k in range(top):
        same = number_f == routes_t[k : k + 1, :]
        named = jnp.where(same, 1.0, named)
        weight = jnp.where(same, gates_t[k : k + 1, :], weight)
    earlier = (iota((tokens, tokens), 0) < iota((tokens, tokens), 1)).astype(F32).astype(BF16)
    slots = dot(named.astype(BF16), earlier)
    base = (lax.rem(number, local) * cap).astype(F32)
    code = jnp.where(named > 0.0, slots + base, -1.0)
    seq_row = seq[...]
    for k in range(ne):
        pick_rows = slice(k * local, (k + 1) * local)
        tbl_mine[k, 0:local, :] = code[pick_rows]
        for s in range(SEQ_DEV):
            tbl_mine[k, (s + 1) * local : (s + 2) * local, :] = jnp.where(
                seq_row == s, weight[pick_rows], 0.0
            )
    for k in range(1, ne):
        table_copy(k).start()
    tbl_all[me] = tbl_mine[me]

    relay(1)

    for k in range(1, nd):
        pin_arrival(k).wait_recv()
    width = pin_all.shape[2]
    for d in range(nd):
        for q in range(quads):
            pin4[q * k_in : (q + 1) * k_in, d * width : (d + 1) * width] = pin_all[d]

    def project(first, last):
        def one(b, carry):
            hidden_copy(b).wait()
            hp[b] = dot_nt(hid[b], pin4[...]).astype(BF16)
            return carry

        lax.fori_loop(first, last, one, 0)

    project(0, ne // 2)
    relay(2)
    project(ne // 2, ne)
    for k in range(1, ne):
        table_arrival(k).wait_recv()
    if far > 2:
        relay(3)

    row = iota((rows, local), 0)
    col = iota((rows, local), 1) * cap
    spread = ((row >= col) & (row < col + cap)).astype(F32).astype(BF16)
    ones = jnp.ones((tokens, LANES), BF16)
    row_f = iota((rows, tokens), 0).astype(F32)
    row_l = iota((rows, LANES), 0)

    def weigh(b, carry):
        placed = dot(spread, tbl_all[b, 0:local, :].astype(BF16)) == row_f
        pick[b] = jnp.where(placed, 1.0, 0.0).astype(BF16)
        stored = hp[b].astype(F32)
        for s in range(SEQ_DEV):
            gates = dot(spread, tbl_all[b, (s + 1) * local : (s + 2) * local, :].astype(BF16))
            amount = dot(jnp.where(placed, gates, 0.0).astype(BF16), ones)
            scaled = stored * amount
            for e in range(local):
                mine = (row_l >= e * cap) & (row_l < (e + 1) * cap)
                first = (s * local + e) * LANES
                bd[b, :, first : first + LANES] = jnp.where(mine, scaled, 0.0).astype(BF16)
        return carry

    own.wait()
    grads.wait()
    aligned = shard % LANES == 0

    def product(source):
        columns = pl.ds(pl.multiple_of(source * shard, LANES), shard)
        block = pl.ds(pl.multiple_of(source * shard, 16), shard)
        return dot(og[:, columns], pall[block, :])

    total = jnp.zeros((tokens, k_out), F32)
    if aligned:
        total = total + product(me)

    def add(total, d):
        handed(d)
        if aligned:
            total = total + product(at(here + d))
            if d < far:
                total = total + product(at(here - d))
        return total

    total = add(total, 1)
    lax.fori_loop(0, ne, weigh, 0)
    for d in range(4, far + 1):
        relay(d)
    for d in range(2, far + 1):
        total = add(total, d)
    if not aligned:
        total = dot(og[...], pall[...])

    r = iota((k_out, k_out), 0)
    wanted = quads * lax.rem(r, groups) + lax.div(r, groups)
    shuffle = (wanted == iota((k_out, k_out), 1)).astype(F32).astype(BF16)
    g_all[me] = dot_nt(shuffle, total.astype(BF16)).astype(BF16)

    def grad_copy(k):
        return exchange((g_all.at[me], g_all.at[me]), g_send, g_recv, k, True)

    def grad_arrival(k):
        return exchange(
            (None, g_all.at[lax.rem(me + ne - k, ne)]), g_send, g_recv, k, False
        )

    for k in range(1, ne):
        grad_copy(k).start()

    quad = lax.div(lax.rem(iota((groups, 2 * LANES), 1), LANES), k_in)

    def out_copy(b):
        return pltpu.make_async_copy(
            outv.at[pl.ds(SEQ_DEV * b, SEQ_DEV)],
            out_hbm.at[pl.ds(SEQ_DEV * b, SEQ_DEV)],
            out_sem.at[b],
        )

    for k in range(ne):
        b = lax.rem(me + ne - k, ne)
        if k:
            grad_arrival(k).wait_recv()
        chosen = dot_nt(g_all[b], pick[b]).astype(BF16)
        for s in range(SEQ_DEV):
            for e in range(0, local, 2):
                first = (s * local + e) * LANES
                full = dot(chosen, bd[b, :, first : first + 2 * LANES])
                value = full[0:groups]
                for q in range(1, quads):
                    value = jnp.where(quad == q, full[q * groups : (q + 1) * groups], value)
                place = s * groups * local + e
                stage[pl.ds(place, groups, stride=local), :] = value[:, :LANES]
                stage[pl.ds(place + 1, groups, stride=local), :] = value[:, LANES:]
            for j in range(groups):
                place = (s * groups + j) * local
                outv[SEQ_DEV * b + s, :, j * LANES : (j + 1) * LANES] = stage[
                    place : place + local, :
                ].astype(BF16)
        out_copy(b).start()

    for k in range(1, ne):
        grad_copy(k).wait_send()
        table_copy(k).wait_send()
    for k in range(1, nd):
        pin_copy(k).wait_send()
    for d in range(1, far + 1):
        for way in (0, 1):
            for part in uses(way, d):
                ring(way, d, part).wait_send()
                hand_over(way, d, part, core).wait_send()
    for b in range(ne):
        out_copy(b).wait()


def shards(nd, ne, out_grad, gate_weights, routes, seq_ids, hidden, proj_out, proj_in):
    blocks, local, cap, width = hidden.shape
    tokens, features = out_grad.shape
    k_out, k_in = proj_out.shape[1], proj_in.shape[1]
    rows = local * cap
    far = ne // 2
    dma = pltpu.SemaphoreType.DMA
    return pl.pallas_call(
        functools.partial(kernel, nd, ne, cap),
        out_shape=jax.ShapeDtypeStruct((blocks * SEQ_DEV, local, k_out * k_in), BF16),
        in_specs=[pl.BlockSpec(memory_space=pl.ANY)] * 7,
        out_specs=pl.BlockSpec(memory_space=pl.ANY),
        scratch_shapes=[
            pltpu.VMEM((tokens, features), BF16),
            pltpu.VMEM(gate_weights.shape, BF16),
            pltpu.VMEM(routes.shape, jnp.int32),
            pltpu.VMEM(seq_ids.shape, jnp.int32),
            pltpu.VMEM((blocks, rows, width), BF16),
            pltpu.VMEM((features, k_out), BF16),
            pltpu.VMEM(proj_in.shape, BF16),
            pltpu.VMEM((nd, k_in, width // nd), BF16),
            pltpu.VMEM((LANES, width), BF16),
            pltpu.VMEM((ne, (SEQ_DEV + 1) * local, tokens), F32),
            pltpu.VMEM((ne, (SEQ_DEV + 1) * local, tokens), F32),
            pltpu.VMEM((ne, k_out, tokens), BF16),
            pltpu.VMEM((ne, rows, LANES), BF16),
            pltpu.VMEM((ne, rows, tokens), BF16),
            pltpu.VMEM((ne, rows, SEQ_DEV * local * LANES), BF16),
            pltpu.VMEM((SEQ_DEV * local * k_out * k_in // LANES, LANES), F32),
            pltpu.VMEM((blocks * SEQ_DEV, local, k_out * k_in), BF16),
            dma, dma((4,)), dma((ne,)), dma,
            dma((2, far, 2)), dma((2, far, 2)), dma((2, far, 2)), dma((2, far, 2)),
            dma((nd - 1,)), dma((nd - 1,)), dma((ne - 1,)), dma((ne - 1,)),
            dma((ne - 1,)), dma((ne - 1,)), dma((ne,)),
        ],
        compiler_params=pltpu.CompilerParams(
            collective_id=0, has_side_effects=True, vmem_limit_bytes=48 * 1024 * 1024
        ),
    )(out_grad, gate_weights, routes, seq_ids, hidden.reshape(-1, width), proj_out, proj_in)


def solution(mesh):
    placed = (
        P(("dp", "expert"), None),
        P(("dp", "expert"), None),
        P(("dp", "expert"), None),
        P(("dp", "expert"), None),
        P("dp", "expert", None, None),
        P("expert", None),
        P("dp", None),
    )
    return jax.shard_map(
        functools.partial(shards, mesh.shape["dp"], mesh.shape["expert"]),
        mesh=mesh,
        in_specs=placed,
        out_specs=P("dp", "expert", None),
        check_vma=False,
    )
```

```python
import functools

import jax
import jax.numpy as jnp
from jax import lax
from jax.experimental import pallas as pl
from jax.experimental.pallas import tpu as pltpu
from jax.sharding import PartitionSpec as P

SEQ_DEV = 2
LANES = 128
MESH = pl.DeviceIdType.MESH
F32 = jnp.float32
BF16 = jnp.bfloat16


def iota(shape, dim):
    return lax.broadcasted_iota(jnp.int32, shape, dim)


def dot(a, b):
    return jnp.dot(a, b, preferred_element_type=F32)


def dot_nt(a, b):
    return lax.dot_general(a, b, (((1,), (1,)), ((), ())), preferred_element_type=F32)


def kernel(
    nd, ne, cap,
    og_hbm, gate_hbm, routes_hbm, seq_hbm, hid_hbm, po_hbm, pi_hbm, outv,
    og, gate, routes, seq, hid, pall, pin_all, pin4, tbl_mine, tbl_all, g_all,
    hp, pick, bd, stage,
    og_sem, small_sem, hid_sem, po_sem, ring_send, ring_recv, sib_send, sib_recv,
    pin_send, pin_recv, tbl_send, tbl_recv, g_send, g_recv,
):
    tokens = og.shape[0]
    shard = po_hbm.shape[0]
    k_out = po_hbm.shape[1]
    k_in = pi_hbm.shape[0]
    top = routes.shape[0]
    rows = hp.shape[1]
    local = rows // cap
    experts = ne * local
    quads = LANES // k_in
    groups = k_out // quads
    half = shard // 2
    cut = half // 32 * 16
    parts = ((0, cut), (cut, half - cut))
    far = ne // 2

    dp = lax.axis_index("dp")
    me = lax.axis_index("expert")
    core = lax.rem(dp, 2)
    sibling = dp + 1 - 2 * core
    odd = lax.rem(me, 2)
    here = (1 - odd) * (me // 2) + odd * (ne - 1 - me // 2)

    def at(place):
        place = lax.rem(place + 2 * ne, ne)
        back = place // (ne // 2)
        return (1 - back) * (2 * place) + back * (2 * (ne - 1 - place) + 1)

    small = [
        pltpu.make_async_copy(pi_hbm, pin_all.at[dp], small_sem.at[0]),
        pltpu.make_async_copy(routes_hbm, routes, small_sem.at[1]),
        pltpu.make_async_copy(gate_hbm, gate, small_sem.at[2]),
        pltpu.make_async_copy(seq_hbm, seq, small_sem.at[3]),
    ]
    own_rows = pl.ds(pl.multiple_of(me * shard, 16), shard)
    own = pltpu.make_async_copy(po_hbm, pall.at[own_rows, :], po_sem)
    grads = pltpu.make_async_copy(og_hbm, og, og_sem)
    for copy in small:
        copy.start()
    own.start()
    grads.start()

    def hidden_copy(b):
        return pltpu.make_async_copy(
            hid_hbm.at[pl.ds(b * rows, rows), :], hid.at[b], hid_sem.at[b]
        )

    for b in range(ne):
        hidden_copy(b).start()

    barrier = pltpu.get_barrier_semaphore()
    for k in range(1, ne):
        pl.semaphore_signal(
            barrier, inc=1, device_id=(dp, lax.rem(me + k, ne)), device_id_type=MESH
        )
    for k in range(1, nd):
        pl.semaphore_signal(
            barrier, inc=1, device_id=(lax.rem(dp + k, nd), me), device_id_type=MESH
        )
    pl.semaphore_wait(barrier, ne + nd - 2)

    def step(way):
        return 1 - 2 * way

    def uses(way, d):
        return (0, 1) if d < far else (way,)

    def span(source, part, side):
        first, size = parts[part]
        return pl.ds(pl.multiple_of(source * shard + side * half + first, 16), size)

    def ring(way, d, part):
        source = at(here - step(way) * (d - 1))
        first, size = parts[part]
        if d == 1:
            src = po_hbm.at[pl.ds(pl.multiple_of(core * half + first, 16), size), :]
        else:
            src = pall.at[span(source, part, core), :]
        return pltpu.make_async_remote_copy(
            src_ref=src,
            dst_ref=pall.at[span(source, part, core), :],
            send_sem=ring_send.at[way, d - 1, part],
            recv_sem=ring_recv.at[way, d - 1, part],
            device_id=(dp, at(here + step(way))),
            device_id_type=MESH,
        )

    def ring_arrival(way, d, part):
        source = at(here - step(way) * d)
        block = pall.at[span(source, part, core), :]
        return pltpu.make_async_remote_copy(
            src_ref=block,
            dst_ref=block,
            send_sem=ring_send.at[way, d - 1, part],
            recv_sem=ring_recv.at[way, d - 1, part],
            device_id=(dp, at(here + step(way))),
            device_id_type=MESH,
        )

    def hand_over(way, d, part, side):
        source = at(here - step(way) * d)
        block = pall.at[span(source, part, side), :]
        return pltpu.make_async_remote_copy(
            src_ref=block,
            dst_ref=block,
            send_sem=sib_send.at[way, d - 1, part],
            recv_sem=sib_recv.at[way, d - 1, part],
            device_id=(sibling, me),
            device_id_type=MESH,
        )

    def relay(d):
        for part in (0, 1):
            for way in (0, 1):
                if part in uses(way, d):
                    ring_arrival(way, d, part).wait_recv()
                    if d < far and part in uses(way, d + 1):
                        ring(way, d + 1, part).start()
                    hand_over(way, d, part, core).start()

    def handed(d):
        for way in (0, 1):
            for part in uses(way, d):
                hand_over(way, d, part, 1 - core).wait_recv()

    for part in (0, 1):
        for way in (0, 1):
            ring(way, 1, part).start()

    def pin_copy(k):
        return pltpu.make_async_remote_copy(
            src_ref=pin_all.at[dp],
            dst_ref=pin_all.at[dp],
            send_sem=pin_send.at[k - 1],
            recv_sem=pin_recv.at[k - 1],
            device_id=(lax.rem(dp + k, nd), me),
            device_id_type=MESH,
        )

    def pin_arrival(k):
        block = pin_all.at[lax.rem(dp + nd - k, nd)]
        return pltpu.make_async_remote_copy(
            src_ref=block,
            dst_ref=block,
            send_sem=pin_send.at[k - 1],
            recv_sem=pin_recv.at[k - 1],
            device_id=(lax.rem(dp + k, nd), me),
            device_id_type=MESH,
        )

    small[0].wait()
    for k in range(1, nd):
        pin_copy(k).start()

    def exchange(buffer, sends, receives, k, mine):
        if mine:
            src, dst = buffer
        else:
            dst = buffer[1]
            src = dst
        return pltpu.make_async_remote_copy(
            src_ref=src,
            dst_ref=dst,
            send_sem=sends.at[k - 1],
            recv_sem=receives.at[k - 1],
            device_id=(dp, lax.rem(me + k, ne)),
            device_id_type=MESH,
        )

    def table_copy(k):
        return exchange(
            (tbl_mine.at[lax.rem(me + k, ne)], tbl_all.at[me]), tbl_send, tbl_recv, k, True
        )

    def table_arrival(k):
        return exchange(
            (None, tbl_all.at[lax.rem(me + ne - k, ne)]), tbl_send, tbl_recv, k, False
        )

    for copy in small[1:]:
        copy.wait()
    routes_t = routes[...]
    gates_t = gate[...].astype(F32)
    number = iota((experts, tokens), 0)
    named = jnp.zeros((experts, tokens), F32)
    weight = jnp.zeros((experts, tokens), F32)
    for k in range(top):
        same = number == routes_t[k : k + 1, :]
        named = jnp.where(same, 1.0, named)
        weight = jnp.where(same, gates_t[k : k + 1, :], weight)
    earlier = (iota((tokens, tokens), 0) < iota((tokens, tokens), 1)).astype(F32).astype(BF16)
    slots = dot(named.astype(BF16), earlier)
    base = (lax.rem(number, local) * cap).astype(F32)
    code = jnp.where(named > 0.0, slots + base, -1.0)
    seq_row = seq[...]
    for k in range(ne):
        pick_rows = slice(k * local, (k + 1) * local)
        tbl_mine[k, 0:local, :] = code[pick_rows]
        for s in range(SEQ_DEV):
            tbl_mine[k, (s + 1) * local : (s + 2) * local, :] = jnp.where(
                seq_row == s, weight[pick_rows], 0.0
            )
    for k in range(1, ne):
        table_copy(k).start()
    tbl_all[me] = tbl_mine[me]

    relay(1)

    for k in range(1, nd):
        pin_arrival(k).wait_recv()
    width = pin_all.shape[2]
    for d in range(nd):
        for q in range(quads):
            pin4[q * k_in : (q + 1) * k_in, d * width : (d + 1) * width] = pin_all[d]

    def project(first, last):
        def one(b, carry):
            hidden_copy(b).wait()
            hp[b] = dot_nt(hid[b], pin4[...]).astype(BF16)
            return carry

        lax.fori_loop(first, last, one, 0)

    project(0, ne // 2)
    relay(2)
    project(ne // 2, ne)
    for k in range(1, ne):
        table_arrival(k).wait_recv()
    if far > 2:
        relay(3)

    row = iota((rows, local), 0)
    col = iota((rows, local), 1) * cap
    spread = ((row >= col) & (row < col + cap)).astype(F32).astype(BF16)
    ones = jnp.ones((tokens, LANES), BF16)
    row_f = iota((rows, tokens), 0).astype(F32)
    row_l = iota((rows, LANES), 0)

    def weigh(b, carry):
        placed = dot(spread, tbl_all[b, 0:local, :].astype(BF16)) == row_f
        pick[b] = jnp.where(placed, 1.0, 0.0).astype(BF16)
        stored = hp[b].astype(F32)
        for s in range(SEQ_DEV):
            gates = dot(spread, tbl_all[b, (s + 1) * local : (s + 2) * local, :].astype(BF16))
            amount = dot(jnp.where(placed, gates, 0.0).astype(BF16), ones)
            scaled = stored * amount
            for e in range(local):
                mine = (row_l >= e * cap) & (row_l < (e + 1) * cap)
                first = (s * local + e) * LANES
                bd[b, :, first : first + LANES] = jnp.where(mine, scaled, 0.0).astype(BF16)
        return carry

    own.wait()
    grads.wait()
    aligned = shard % LANES == 0

    def product(source):
        columns = pl.ds(pl.multiple_of(source * shard, LANES), shard)
        block = pl.ds(pl.multiple_of(source * shard, 16), shard)
        return dot(og[:, columns], pall[block, :])

    total = jnp.zeros((tokens, k_out), F32)
    if aligned:
        total = total + product(me)

    def add(total, d):
        handed(d)
        if aligned:
            total = total + product(at(here + d))
            if d < far:
                total = total + product(at(here - d))
        return total

    total = add(total, 1)
    lax.fori_loop(0, ne, weigh, 0)
    for d in range(4, far + 1):
        relay(d)
    for d in range(2, far + 1):
        total = add(total, d)
    if not aligned:
        total = dot(og[...], pall[...])

    r = iota((k_out, k_out), 0)
    wanted = quads * lax.rem(r, groups) + lax.div(r, groups)
    shuffle = (wanted == iota((k_out, k_out), 1)).astype(F32).astype(BF16)
    g_all[me] = dot_nt(shuffle, total.astype(BF16)).astype(BF16)

    def grad_copy(k):
        return exchange((g_all.at[me], g_all.at[me]), g_send, g_recv, k, True)

    def grad_arrival(k):
        return exchange(
            (None, g_all.at[lax.rem(me + ne - k, ne)]), g_send, g_recv, k, False
        )

    for k in range(1, ne):
        grad_copy(k).start()

    quad = lax.div(lax.rem(iota((groups, 2 * LANES), 1), LANES), k_in)

    for k in range(ne):
        b = lax.rem(me + ne - k, ne)
        if k:
            grad_arrival(k).wait_recv()
        chosen = dot_nt(g_all[b], pick[b]).astype(BF16)
        for s in range(SEQ_DEV):
            for e in range(0, local, 2):
                first = (s * local + e) * LANES
                full = dot(chosen, bd[b, :, first : first + 2 * LANES])
                value = full[0:groups]
                for q in range(1, quads):
                    value = jnp.where(quad == q, full[q * groups : (q + 1) * groups], value)
                place = s * groups * local + e
                stage[pl.ds(place, groups, stride=local), :] = value[:, :LANES]
                stage[pl.ds(place + 1, groups, stride=local), :] = value[:, LANES:]
            for j in range(groups):
                place = (s * groups + j) * local
                outv[SEQ_DEV * b + s, :, j * LANES : (j + 1) * LANES] = stage[
                    place : place + local, :
                ].astype(BF16)

    for k in range(1, ne):
        grad_copy(k).wait_send()
        table_copy(k).wait_send()
    for k in range(1, nd):
        pin_copy(k).wait_send()
    for d in range(1, far + 1):
        for way in (0, 1):
            for part in uses(way, d):
                ring(way, d, part).wait_send()
                hand_over(way, d, part, core).wait_send()


def shards(nd, ne, out_grad, gate_weights, routes, seq_ids, hidden, proj_out, proj_in):
    blocks, local, cap, width = hidden.shape
    tokens, features = out_grad.shape
    k_out, k_in = proj_out.shape[1], proj_in.shape[1]
    rows = local * cap
    far = ne // 2
    dma = pltpu.SemaphoreType.DMA
    return pl.pallas_call(
        functools.partial(kernel, nd, ne, cap),
        out_shape=jax.ShapeDtypeStruct((blocks * SEQ_DEV, local, k_out * k_in), BF16),
        in_specs=[pl.BlockSpec(memory_space=pltpu.HBM)] * 7,
        out_specs=pl.BlockSpec(memory_space=pltpu.VMEM),
        scratch_shapes=[
            pltpu.VMEM((tokens, features), BF16),
            pltpu.VMEM(gate_weights.shape[::-1], BF16),
            pltpu.VMEM(routes.shape[::-1], jnp.int32),
            pltpu.VMEM(seq_ids.shape, jnp.int32),
            pltpu.VMEM((blocks, rows, width), BF16),
            pltpu.VMEM((features, k_out), BF16),
            pltpu.VMEM((nd, k_in, width // nd), BF16),
            pltpu.VMEM((LANES, width), BF16),
            pltpu.VMEM((ne, (SEQ_DEV + 1) * local, tokens), F32),
            pltpu.VMEM((ne, (SEQ_DEV + 1) * local, tokens), F32),
            pltpu.VMEM((ne, k_out, tokens), BF16),
            pltpu.VMEM((ne, rows, LANES), BF16),
            pltpu.VMEM((ne, rows, tokens), BF16),
            pltpu.VMEM((ne, rows, SEQ_DEV * local * LANES), BF16),
            pltpu.VMEM((SEQ_DEV * local * k_out * k_in // LANES, LANES), F32),
            dma, dma((4,)), dma((ne,)), dma,
            dma((2, far, 2)), dma((2, far, 2)), dma((2, far, 2)), dma((2, far, 2)),
            dma((nd - 1,)), dma((nd - 1,)), dma((ne - 1,)), dma((ne - 1,)),
            dma((ne - 1,)), dma((ne - 1,)),
        ],
        compiler_params=pltpu.CompilerParams(
            collective_id=0, has_side_effects=True, vmem_limit_bytes=63 * 1024 * 1024 + 512 * 1024
        ),
    )(
        out_grad, gate_weights.T, routes.T, seq_ids, hidden.reshape(-1, width), proj_out, proj_in.T
    )


def solution(mesh):
    placed = (
        P(("dp", "expert"), None),
        P(("dp", "expert"), None),
        P(("dp", "expert"), None),
        P(("dp", "expert"), None),
        P("dp", "expert", None, None),
        P("expert", None),
        P("dp", None),
    )
    return jax.shard_map(
        functools.partial(shards, mesh.shape["dp"], mesh.shape["expert"]),
        mesh=mesh,
        in_specs=placed,
        out_specs=P("dp", "expert", None),
        check_vma=False,
    )
```

```python
import functools

import jax
import jax.numpy as jnp
from jax import lax
from jax.experimental import pallas as pl
from jax.experimental.pallas import tpu as pltpu
from jax.sharding import PartitionSpec as P

SEQ_DEV = 2
LANES = 128
MESH = pl.DeviceIdType.MESH
F32 = jnp.float32
BF16 = jnp.bfloat16


def iota(shape, dim):
    return lax.broadcasted_iota(jnp.int32, shape, dim)


def dot(a, b):
    return jnp.dot(a, b, preferred_element_type=F32)


def dot_nt(a, b):
    return lax.dot_general(a, b, (((1,), (1,)), ((), ())), preferred_element_type=F32)


def kernel(
    nd, ne, cap,
    og_hbm, gate_hbm, routes_hbm, seq_hbm, hid_hbm, po_hbm, pi_hbm, outv,
    og, gate, routes, seq, hid, pall, pin_all, pin4, tbl_mine, tbl_all, g_all,
    hp, pick, bd, stage,
    og_sem, small_sem, hid_sem, po_sem, ring_send, ring_recv, sib_send, sib_recv,
    pin_send, pin_recv, tbl_send, tbl_recv, g_send, g_recv,
):
    tokens = og.shape[0]
    shard = po_hbm.shape[0]
    k_out = po_hbm.shape[1]
    k_in = pi_hbm.shape[0]
    top = routes.shape[0]
    rows = hp.shape[1]
    local = rows // cap
    experts = ne * local
    quads = LANES // k_in
    groups = k_out // quads
    half = shard // 2
    cut = half // 32 * 16
    parts = ((0, cut), (cut, half - cut))
    far = ne // 2

    dp = lax.axis_index("dp")
    me = lax.axis_index("expert")
    core = lax.rem(dp, 2)
    sibling = dp + 1 - 2 * core
    odd = lax.rem(me, 2)
    here = (1 - odd) * (me // 2) + odd * (ne - 1 - me // 2)

    def at(place):
        place = lax.rem(place + 2 * ne, ne)
        back = place // (ne // 2)
        return (1 - back) * (2 * place) + back * (2 * (ne - 1 - place) + 1)

    small = [
        pltpu.make_async_copy(pi_hbm, pin_all.at[dp], small_sem.at[0]),
        pltpu.make_async_copy(routes_hbm, routes, small_sem.at[1]),
        pltpu.make_async_copy(gate_hbm, gate, small_sem.at[2]),
        pltpu.make_async_copy(seq_hbm, seq, small_sem.at[3]),
    ]
    own_rows = pl.ds(pl.multiple_of(me * shard, 16), shard)
    own = pltpu.make_async_copy(po_hbm, pall.at[own_rows, :], po_sem)
    grads = pltpu.make_async_copy(og_hbm, og, og_sem)
    for copy in small:
        copy.start()
    own.start()
    grads.start()

    def hidden_copy(b):
        return pltpu.make_async_copy(
            hid_hbm.at[pl.ds(b * rows, rows), :], hid.at[b], hid_sem.at[b]
        )

    for b in range(ne):
        hidden_copy(b).start()

    barrier = pltpu.get_barrier_semaphore()
    for k in range(1, ne):
        pl.semaphore_signal(
            barrier, inc=1, device_id=(dp, lax.rem(me + k, ne)), device_id_type=MESH
        )
    for k in range(1, nd):
        pl.semaphore_signal(
            barrier, inc=1, device_id=(lax.rem(dp + k, nd), me), device_id_type=MESH
        )
    pl.semaphore_wait(barrier, ne + nd - 2)

    def step(way):
        return 1 - 2 * way

    def uses(way, d):
        return (0, 1) if d < far else (way,)

    def span(source, part, side):
        first, size = parts[part]
        return pl.ds(pl.multiple_of(source * shard + side * half + first, 16), size)

    def ring(way, d, part):
        source = at(here - step(way) * (d - 1))
        first, size = parts[part]
        if d == 1:
            src = po_hbm.at[pl.ds(pl.multiple_of(core * half + first, 16), size), :]
        else:
            src = pall.at[span(source, part, core), :]
        return pltpu.make_async_remote_copy(
            src_ref=src,
            dst_ref=pall.at[span(source, part, core), :],
            send_sem=ring_send.at[way, d - 1, part],
            recv_sem=ring_recv.at[way, d - 1, part],
            device_id=(dp, at(here + step(way))),
            device_id_type=MESH,
        )

    def ring_arrival(way, d, part):
        source = at(here - step(way) * d)
        block = pall.at[span(source, part, core), :]
        return pltpu.make_async_remote_copy(
            src_ref=block,
            dst_ref=block,
            send_sem=ring_send.at[way, d - 1, part],
            recv_sem=ring_recv.at[way, d - 1, part],
            device_id=(dp, at(here + step(way))),
            device_id_type=MESH,
        )

    def hand_over(way, d, part, side):
        source = at(here - step(way) * d)
        block = pall.at[span(source, part, side), :]
        return pltpu.make_async_remote_copy(
            src_ref=block,
            dst_ref=block,
            send_sem=sib_send.at[way, d - 1, part],
            recv_sem=sib_recv.at[way, d - 1, part],
            device_id=(sibling, me),
            device_id_type=MESH,
        )

    def relay(d):
        for part in (0, 1):
            for way in (0, 1):
                if part in uses(way, d):
                    ring_arrival(way, d, part).wait_recv()
                    if d < far and part in uses(way, d + 1):
                        ring(way, d + 1, part).start()
                    hand_over(way, d, part, core).start()

    def handed(d):
        for way in (0, 1):
            for part in uses(way, d):
                hand_over(way, d, part, 1 - core).wait_recv()

    for part in (0, 1):
        for way in (0, 1):
            ring(way, 1, part).start()

    def pin_copy(k):
        return pltpu.make_async_remote_copy(
            src_ref=pin_all.at[dp],
            dst_ref=pin_all.at[dp],
            send_sem=pin_send.at[k - 1],
            recv_sem=pin_recv.at[k - 1],
            device_id=(lax.rem(dp + k, nd), me),
            device_id_type=MESH,
        )

    def pin_arrival(k):
        block = pin_all.at[lax.rem(dp + nd - k, nd)]
        return pltpu.make_async_remote_copy(
            src_ref=block,
            dst_ref=block,
            send_sem=pin_send.at[k - 1],
            recv_sem=pin_recv.at[k - 1],
            device_id=(lax.rem(dp + k, nd), me),
            device_id_type=MESH,
        )

    small[0].wait()
    for k in range(1, nd):
        pin_copy(k).start()

    def exchange(buffer, sends, receives, k, mine):
        if mine:
            src, dst = buffer
        else:
            dst = buffer[1]
            src = dst
        return pltpu.make_async_remote_copy(
            src_ref=src,
            dst_ref=dst,
            send_sem=sends.at[k - 1],
            recv_sem=receives.at[k - 1],
            device_id=(dp, lax.rem(me + k, ne)),
            device_id_type=MESH,
        )

    def table_copy(k):
        return exchange(
            (tbl_mine.at[lax.rem(me + k, ne)], tbl_all.at[me]), tbl_send, tbl_recv, k, True
        )

    def table_arrival(k):
        return exchange(
            (None, tbl_all.at[lax.rem(me + ne - k, ne)]), tbl_send, tbl_recv, k, False
        )

    for copy in small[1:]:
        copy.wait()
    routes_t = routes[...]
    gates_t = gate[...].astype(F32)
    number = iota((experts, tokens), 0)
    named = jnp.zeros((experts, tokens), F32)
    weight = jnp.zeros((experts, tokens), F32)
    for k in range(top):
        same = number == routes_t[k : k + 1, :]
        named = jnp.where(same, 1.0, named)
        weight = jnp.where(same, gates_t[k : k + 1, :], weight)
    earlier = (iota((tokens, tokens), 0) < iota((tokens, tokens), 1)).astype(F32).astype(BF16)
    slots = dot(named.astype(BF16), earlier)
    base = (lax.rem(number, local) * cap).astype(F32)
    code = jnp.where(named > 0.0, slots + base, -1.0)
    seq_row = seq[...]
    for k in range(ne):
        pick_rows = slice(k * local, (k + 1) * local)
        tbl_mine[k, 0:local, :] = code[pick_rows]
        for s in range(SEQ_DEV):
            tbl_mine[k, (s + 1) * local : (s + 2) * local, :] = jnp.where(
                seq_row == s, weight[pick_rows], 0.0
            )
    for k in range(1, ne):
        table_copy(k).start()
    tbl_all[me] = tbl_mine[me]

    relay(1)

    for k in range(1, nd):
        pin_arrival(k).wait_recv()
    width = pin_all.shape[2]
    for d in range(nd):
        for q in range(quads):
            pin4[q * k_in : (q + 1) * k_in, d * width : (d + 1) * width] = pin_all[d]

    def project(first, last):
        def one(b, carry):
            hidden_copy(b).wait()
            hp[b] = dot_nt(hid[b], pin4[...]).astype(BF16)
            return carry

        lax.fori_loop(first, last, one, 0)

    project(0, ne // 2)
    relay(2)
    project(ne // 2, ne)
    for k in range(1, ne):
        table_arrival(k).wait_recv()
    if far > 2:
        relay(3)

    row = iota((rows, local), 0)
    col = iota((rows, local), 1) * cap
    spread = ((row >= col) & (row < col + cap)).astype(F32).astype(BF16)
    ones = jnp.ones((tokens, LANES), BF16)
    row_f = iota((rows, tokens), 0).astype(F32)
    row_l = iota((rows, LANES), 0)

    def weigh(b, carry):
        placed = dot(spread, tbl_all[b, 0:local, :].astype(BF16)) == row_f
        pick[b] = jnp.where(placed, 1.0, 0.0).astype(BF16)
        stored = hp[b].astype(F32)
        for s in range(SEQ_DEV):
            gates = dot(spread, tbl_all[b, (s + 1) * local : (s + 2) * local, :].astype(BF16))
            amount = dot(jnp.where(placed, gates, 0.0).astype(BF16), ones)
            scaled = stored * amount
            for e in range(local):
                mine = (row_l >= e * cap) & (row_l < (e + 1) * cap)
                first = (s * local + e) * LANES
                bd[b, :, first : first + LANES] = jnp.where(mine, scaled, 0.0).astype(BF16)
        return carry

    own.wait()
    grads.wait()
    aligned = shard % LANES == 0

    def product(source):
        columns = pl.ds(pl.multiple_of(source * shard, LANES), shard)
        block = pl.ds(pl.multiple_of(source * shard, 16), shard)
        return dot(og[:, columns], pall[block, :])

    total = jnp.zeros((tokens, k_out), F32)
    if aligned:
        total = total + product(me)

    def add(total, d):
        handed(d)
        if aligned:
            total = total + product(at(here + d))
            if d < far:
                total = total + product(at(here - d))
        return total

    total = add(total, 1)
    lax.fori_loop(0, ne, weigh, 0)
    for d in range(4, far + 1):
        relay(d)
    for d in range(2, far + 1):
        total = add(total, d)
    if not aligned:
        total = dot(og[...], pall[...])

    r = iota((k_out, k_out), 0)
    wanted = quads * lax.rem(r, groups) + lax.div(r, groups)
    shuffle = (wanted == iota((k_out, k_out), 1)).astype(F32).astype(BF16)
    g_all[me] = dot_nt(shuffle, total.astype(BF16)).astype(BF16)

    def grad_copy(k):
        return exchange((g_all.at[me], g_all.at[me]), g_send, g_recv, k, True)

    def grad_arrival(k):
        return exchange(
            (None, g_all.at[lax.rem(me + ne - k, ne)]), g_send, g_recv, k, False
        )

    for k in range(1, ne):
        grad_copy(k).start()

    quad = lax.div(lax.rem(iota((groups, 2 * LANES), 1), LANES), k_in)

    for k in range(ne):
        b = lax.rem(me + ne - k, ne)
        if k:
            grad_arrival(k).wait_recv()
        chosen = dot_nt(g_all[b], pick[b]).astype(BF16)
        for s in range(SEQ_DEV):
            for e in range(0, local, 2):
                first = (s * local + e) * LANES
                full = dot(chosen, bd[b, :, first : first + 2 * LANES])
                value = full[0:groups]
                for q in range(1, quads):
                    value = jnp.where(quad == q, full[q * groups : (q + 1) * groups], value)
                place = s * groups * local + e
                stage[pl.ds(place, groups, stride=local), :] = value[:, :LANES]
                stage[pl.ds(place + 1, groups, stride=local), :] = value[:, LANES:]
            for j in range(groups):
                place = (s * groups + j) * local
                outv[SEQ_DEV * b + s, :, j * LANES : (j + 1) * LANES] = stage[
                    place : place + local, :
                ].astype(BF16)

    for k in range(1, ne):
        grad_copy(k).wait_send()
        table_copy(k).wait_send()
    for k in range(1, nd):
        pin_copy(k).wait_send()
    for d in range(1, far + 1):
        for way in (0, 1):
            for part in uses(way, d):
                ring(way, d, part).wait_send()
                hand_over(way, d, part, core).wait_send()


def shards(nd, ne, out_grad, gate_weights, routes, seq_ids, hidden, proj_out, proj_in):
    blocks, local, cap, width = hidden.shape
    tokens, features = out_grad.shape
    k_out, k_in = proj_out.shape[1], proj_in.shape[1]
    rows = local * cap
    far = ne // 2
    dma = pltpu.SemaphoreType.DMA
    return pl.pallas_call(
        functools.partial(kernel, nd, ne, cap),
        out_shape=pltpu.VMEM((blocks * SEQ_DEV, local, k_out * k_in), BF16),
        in_specs=[pl.BlockSpec(memory_space=pltpu.HBM)] * 7,
        out_specs=pl.BlockSpec(memory_space=pltpu.VMEM),
        scratch_shapes=[
            pltpu.VMEM((tokens, features), BF16),
            pltpu.VMEM(gate_weights.shape[::-1], BF16),
            pltpu.VMEM(routes.shape[::-1], jnp.int32),
            pltpu.VMEM(seq_ids.shape, jnp.int32),
            pltpu.VMEM((blocks, rows, width), BF16),
            pltpu.VMEM((features, k_out), BF16),
            pltpu.VMEM((nd, k_in, width // nd), BF16),
            pltpu.VMEM((LANES, width), BF16),
            pltpu.VMEM((ne, (SEQ_DEV + 1) * local, tokens), F32),
            pltpu.VMEM((ne, (SEQ_DEV + 1) * local, tokens), F32),
            pltpu.VMEM((ne, k_out, tokens), BF16),
            pltpu.VMEM((ne, rows, LANES), BF16),
            pltpu.VMEM((ne, rows, tokens), BF16),
            pltpu.VMEM((ne, rows, SEQ_DEV * local * LANES), BF16),
            pltpu.VMEM((SEQ_DEV * local * k_out * k_in // LANES, LANES), F32),
            dma, dma((4,)), dma((ne,)), dma,
            dma((2, far, 2)), dma((2, far, 2)), dma((2, far, 2)), dma((2, far, 2)),
            dma((nd - 1,)), dma((nd - 1,)), dma((ne - 1,)), dma((ne - 1,)),
            dma((ne - 1,)), dma((ne - 1,)),
        ],
        compiler_params=pltpu.CompilerParams(
            collective_id=0, has_side_effects=True, vmem_limit_bytes=56 * 1024 * 1024
        ),
    )(
        out_grad, gate_weights.T, routes.T, seq_ids, hidden.reshape(-1, width), proj_out, proj_in.T
    )


def solution(mesh):
    placed = (
        P(("dp", "expert"), None),
        P(("dp", "expert"), None),
        P(("dp", "expert"), None),
        P(("dp", "expert"), None),
        P("dp", "expert", None, None),
        P("expert", None),
        P("dp", None),
    )
    return jax.shard_map(
        functools.partial(shards, mesh.shape["dp"], mesh.shape["expert"]),
        mesh=mesh,
        in_specs=placed,
        out_specs=P("dp", "expert", None),
        check_vma=False,
    )
```
